32 devices in a mesh: dp: 8 (over z, y), tensor: 4 (over x, core).
Axes of the slice: x: 2, y: 2, z: 4, core: 2. Of those that a mesh axis runs over, the one named last changes fastest.
Arguments:
- stream: float32 [8192, 1024], P(('dp', 'tensor')), may hold values from -6 to 6
- cotangent: float32 [8192, 1024], P(('dp', 'tensor')), may hold values from -15 to 15
- lengths: int32 [8, 3], P('dp'), may hold values from 1 to 896, 1024 in all within a row
- routes: int32 [8192, 8], P('dp'), may hold values from 0 to 31, all different within a row; in each aligned block of 1024 rows (0 to 1023, 1024 to 2047, ...) at most 512 rows name the same one
- query_weight: float32 [1024, 1024], P('dp', 'tensor'), may hold values from -0.1875 to 0.1875
- query_moment: float32 [1024, 1024], P('dp', 'tensor'), may hold values from -96 to 96
- query_second: float32 [1024, 1024], P('dp', 'tensor'), may hold values from 983.04 to 3932.16
- key_value_weight: float32 [2, 1024, 512], P(None, 'dp', 'tensor'), may hold values from -0.1875 to 0.1875
- key_value_moment: float32 [2, 1024, 512], P(None, 'dp', 'tensor'), may hold values from -96 to 96
- key_value_second: float32 [2, 1024, 512], P(None, 'dp', 'tensor'), may hold values from 983.04 to 3932.16
- output_weight: float32 [1024, 1024], P('tensor', 'dp'), may hold values from -4 to 4
- output_moment: float32 [1024, 1024], P('tensor', 'dp'), may hold values from -6 to 6
- output_second: float32 [1024, 1024], P('tensor', 'dp'), may hold values from 3.6 to 14.4
- router_weight: float32 [1024, 32], replicated, may hold values from -0.09375 to 0.09375
- router_moment: float32 [1024, 32], replicated, may hold values from -512 to 512
- router_second: float32 [1024, 32], replicated, may hold values from 31129.6 to 124518.4
- gate_up_weight: float32 [2, 32, 1024, 512], P(None, None, 'dp', 'tensor'), may hold values from -0.1875 to 0.1875
- gate_up_moment: float32 [2, 32, 1024, 512], P(None, None, 'dp', 'tensor'), may hold values from -20 to 20
- gate_up_second: float32 [2, 32, 1024, 512], P(None, None, 'dp', 'tensor'), may hold values from 41.6 to 166.4
- down_weight: float32 [32, 512, 1024], P(None, 'tensor', 'dp'), may hold values from -1 to 1
- down_moment: float32 [32, 512, 1024], P(None, 'tensor', 'dp'), may hold values from -4 to 4
- down_second: float32 [32, 512, 1024], P(None, 'tensor', 'dp'), may hold values from 1.76 to 7.04
- norm_gains: float32 [2, 1024], replicated, may hold values from 0.5 to 1.5
- gains_moment: float32 [2, 1024], replicated, may hold values from -128 to 128
- gains_second: float32 [2, 1024], replicated, may hold values from 2048 to 8192
Outputs:
- result: float32 [8192, 1024], P(('dp', 'tensor'))
- stream_grad: float32 [8192, 1024], P(('dp', 'tensor'))
- new_query_moment: float32 [1024, 1024], P('dp', 'tensor')
- new_query_second: float32 [1024, 1024], P('dp', 'tensor')
- new_query_weight: float32 [1024, 1024], P('dp', 'tensor')
- new_key_value_moment: float32 [2, 1024, 512], P(None, 'dp', 'tensor')
- new_key_value_second: float32 [2, 1024, 512], P(None, 'dp', 'tensor')
- new_key_value_weight: float32 [2, 1024, 512], P(None, 'dp', 'tensor')
- new_output_moment: float32 [1024, 1024], P('tensor', 'dp')
- new_output_second: float32 [1024, 1024], P('tensor', 'dp')
- new_output_weight: float32 [1024, 1024], P('tensor', 'dp')
- new_router_moment: float32 [1024, 32], replicated
- new_router_second: float32 [1024, 32], replicated
- new_router_weight: float32 [1024, 32], replicated
- new_gate_up_moment: float32 [2, 32, 1024, 512], P(None, None, 'dp', 'tensor')
- new_gate_up_second: float32 [2, 32, 1024, 512], P(None, None, 'dp', 'tensor')
- new_gate_up_weight: float32 [2, 32, 1024, 512], P(None, None, 'dp', 'tensor')
- new_down_moment: float32 [32, 512, 1024], P(None, 'tensor', 'dp')
- new_down_second: float32 [32, 512, 1024], P(None, 'tensor', 'dp')
- new_down_weight: float32 [32, 512, 1024], P(None, 'tensor', 'dp')
- new_gains_moment: float32 [2, 1024], replicated
- new_gains_second: float32 [2, 1024], replicated
- new_norm_gains: float32 [2, 1024], replicated
The draws below stay inside these ranges and needn't reach their ends.
Inputs may be any that keep to these rules, and one draw needn't show every extreme that they name: `lengths`: the longest sequence of each group has exactly 896 tokens. `routes`: each token names 8 different experts; within each aligned block of 1024 rows (one group) no expert is named by more than 512 rows, and in some block some expert is named by exactly 512.
All inputs are finite; a program needn't handle non-finite values.
Results may differ from the reference program's by a relative error of at most 0.015.
The reference program's roundings to bfloat16 on the way count: a program that leaves them out, or rounds other values in their place, can miss the bound.
Values may be sent and summed in bfloat16 or wider, within the bound.
No kernel may reach another device: no remote copies, remote signals or barrier semaphores. Data moves between devices by JAX's collectives and lax.ppermute only.
A program may use at most 320 MiB of HBM per device.

```python
import math
import jax
import jax.numpy as jnp
import numpy as np
from jax import lax

D = 1024
H = 16
KVH = 8
HD = 64
E = 32
FF = 512
TOP = 8
TOK_DEV = 256
SEQS = 3
STEP = 10
TOK_DP = 1024
TOKENS = 8192
SEQ_MOST = 896
CAP = 512
N_DP = 8


def draw_cotangent(key, part):
    key = jax.random.fold_in(key, 7)
    row_index = jnp.arange(TOKENS, dtype=jnp.int32)
    group_place = (row_index // TOK_DP).astype(jnp.float32) / max(TOKENS // TOK_DP - 1, 1)
    piece_place = (row_index % TOK_DP // TOK_DEV).astype(jnp.float32) / max(TOK_DP // TOK_DEV - 1, 1)
    spread = 0.4 * (1.0 + 2.0 * group_place) * (1.0 + 2.0 * piece_place)
    noise_draw = jax.random.truncated_normal(key, -4.0, 4.0, (TOKENS, D), jnp.float32)
    return noise_draw * spread[:, None]


def shard_levels(own_key, dims, cuts, smallest, high):
    loudness = 1.0
    for dim, parts in cuts:
        heights = jax.random.uniform(jax.random.fold_in(jax.random.fold_in(own_key, 6), dim), (parts,), jnp.float32, smallest / len(cuts), high / len(cuts))
        loudness = loudness * jnp.repeat(jnp.exp(heights), dims[dim] // parts).reshape((-1,) + (1,) * (len(dims) - 1 - dim))
    return loudness


def profile(count, total, limit, slope):
    portions = [(1 << 20) // math.isqrt(grade ** slope) + 1 for grade in range(2, count + 1)]
    rest, given = total - limit - (count - 1), [1] * (count - 1)
    while rest > 0:
        free = [i for i in range(count - 1) if given[i] < limit]
        pool, remaining = sum([portions[i] for i in free]), rest
        for i in free:
            extra = min(limit - given[i], max(1, remaining * portions[i] // pool), rest)
            given[i] = given[i] + extra
            rest = rest - extra
    return np.array([limit] + given)


def uneven(stream_key, count, total, limit, skew):
    if count == 2:
        one = jax.random.randint(stream_key, (), max(1, total - limit), min(limit, total - 1) + 1)
        return jnp.stack([one, total - one])
    tallies = jnp.asarray(profile(count, total, limit, skew), jnp.int32)
    twos = (count - 1) // 2
    source_of, receiver = tallies[1:1 + 2 * twos:2], tallies[2:2 + 2 * twos:2]
    room = jnp.minimum(source_of - 1, limit - receiver)
    moved = jax.random.randint(jax.random.fold_in(stream_key, 1), (twos,), 0, 1 << 20) % (room + 1)
    tallies = tallies.at[1:1 + 2 * twos:2].set(source_of - moved).at[2:2 + 2 * twos:2].set(receiver + moved)
    return tallies[jax.random.permutation(jax.random.fold_in(stream_key, 2), count)]


def routed_block(key, own, number, rows, number_of, top, reach, lean):
    sequence = jax.random.permutation(key, number_of)
    crowded, ordinary = portions_of(number_of, rows * top, reach, lean, True), portions_of(number_of, rows * top, reach, lean, False)
    places = jnp.arange(number_of)

    def named(tallies, offset_by):
        used = int((tallies > 0).sum())
        fixed = max(1, used // 4)
        moved = fixed + (places - fixed + offset_by * (used - fixed)) % max(1, number_of - fixed)
        return jnp.zeros((number_of,), jnp.int32).at[sequence[jnp.where(places < fixed, places, moved)]].set(jnp.asarray(tallies, jnp.int32))

    tallies = jnp.where(number % 4 == 0, named(crowded, number // 4), named(ordinary, number - number // 4 - 1))
    mixed = jax.random.permutation(jax.random.fold_in(own, 3), number_of)
    source_of, receiver = mixed[0:number_of // 2 * 2:2], mixed[1:number_of // 2 * 2:2]
    slack = jnp.minimum(tallies[source_of] - 1, reach - tallies[receiver]) // 2
    slack = jnp.where((source_of == sequence[0]) | (receiver == sequence[0]) | (tallies[receiver] == 0), 0, jnp.maximum(slack, 0))
    moved = jax.random.randint(jax.random.fold_in(own, 4), (number_of // 2,), 0, 1 << 20) % (slack + 1)
    tallies = tallies.at[source_of].add(-moved).at[receiver].add(moved)
    items = jnp.searchsorted(jnp.cumsum(tallies), jnp.arange(rows * top), side="right").astype(jnp.int32)
    table = items.reshape(top, rows).T
    table = table[jax.random.permutation(jax.random.fold_in(own, 1), rows)]
    offset_by = jax.random.randint(jax.random.fold_in(own, 2), (rows, 1), 0, top)
    return jnp.take_along_axis(table, (jnp.arange(top)[None, :] + offset_by) % top, axis=1)


def portions_of(amount, total, limit, slope, full):
    weights = [(1 << 20) // math.isqrt(rank ** slope) + 1 for rank in range(1, amount + 1)]
    largest = limit if full else min(limit, max(-(-total // amount), total * weights[0] // sum(weights)))
    least = 1 if total - largest >= amount - 1 else 0
    counts, rest = [largest] + [least] * (amount - 1), total - largest - least * (amount - 1)
    while rest > 0:
        free = [i for i in range(1, amount) if counts[i] < largest] or [i for i in range(1, amount) if counts[i] < limit]
        pool, budget = sum([weights[i] for i in free]), rest
        for i in free:
            more = min(limit - counts[i], max(1, budget * weights[i] // pool), rest)
            counts[i] = counts[i] + more
            rest = rest - more
    return np.array(counts)


def normal_values(own_key, extent, deviation, bound, shards=(), kind=jnp.bfloat16):
    drawn = deviation * jax.random.normal(own_key, extent, jnp.float32)
    if shards:
        drawn = drawn * shard_levels(own_key, extent, shards, -0.22, 0.18)
    return jnp.clip(drawn, -bound, bound).astype(kind)


def setup_inputs(seed: int = 0) -> dict:
    keys = jax.random.split(jax.random.key(seed), 26)
    stream = normal_values(keys[0], (TOKENS, D), 1.0, 6.0, ((0, 32),), jnp.float32)
    cotangent = draw_cotangent(jax.random.fold_in(keys[25], 71), 0)
    lengths = jax.vmap(lambda own: uneven(own, SEQS, TOK_DP, SEQ_MOST, 2))(jax.random.split(keys[2], N_DP)).reshape((N_DP, SEQS)).astype(jnp.int32)
    routes_keys = jax.random.split(jax.random.fold_in(keys[3], 1), TOKENS // TOK_DP)
    routes_turns = jax.random.permutation(jax.random.fold_in(keys[3], 3), TOKENS // TOK_DP)
    routes = jax.vmap(lambda own, number: routed_block(jax.random.fold_in(keys[3], 2), own, number, TOK_DP, E, TOP, CAP, 1))(routes_keys, routes_turns).reshape((TOKENS, TOP))
    query_weight = normal_values(keys[4], (D, H * HD), D ** -0.5, 0.1875, ((0, 8), (1, 4)), jnp.float32)
    query_moment = normal_values(keys[5], (D, H * HD), (0.17 * TOKENS ** 0.5), 96.0, ((0, 8), (1, 4)), jnp.float32)
    query_second = jnp.clip(jnp.exp(math.log(3932.16) - 1.3862944 * jax.random.uniform(keys[6], (D, H * HD), jnp.float32) ** shard_levels(keys[6], (D, H * HD), ((0, 8), (1, 4)), -0.2, 0.2)), 983.04, 3932.16)
    key_value_weight = normal_values(keys[7], (2, D, KVH * HD), D ** -0.5, 0.1875, ((1, 8), (2, 4)), jnp.float32)
    key_value_moment = normal_values(keys[8], (2, D, KVH * HD), (0.17 * TOKENS ** 0.5), 96.0, ((1, 8), (2, 4)), jnp.float32)
    key_value_second = jnp.clip(jnp.exp(math.log(3932.16) - 1.3862944 * jax.random.uniform(keys[9], (2, D, KVH * HD), jnp.float32) ** shard_levels(keys[9], (2, D, KVH * HD), ((1, 8), (2, 4)), -0.2, 0.2)), 983.04, 3932.16)
    output_weight = normal_values(keys[10], (H * HD, D), (max(1, 2 * H * HD // TOK_DP)) ** -0.5, 4.0, ((0, 4), (1, 8)), jnp.float32)
    output_moment = normal_values(keys[11], (H * HD, D), (0.33 * N_DP ** 0.5), 6.0, ((0, 4), (1, 8)), jnp.float32)
    output_second = jnp.clip(jnp.exp(math.log(14.4) - 1.3862944 * jax.random.uniform(keys[12], (H * HD, D), jnp.float32) ** shard_levels(keys[12], (H * HD, D), ((0, 4), (1, 8)), -0.2, 0.2)), 3.6, 14.4)
    router_weight = normal_values(keys[13], (D, E), (4 * D) ** -0.5, 0.09375, (), jnp.float32)
    router_moment = normal_values(keys[14], (D, E), (0.48 * (D * TOKENS // (TOP * E)) ** 0.5), 512.0, (), jnp.float32)
    router_second = jnp.clip(jnp.exp(jax.random.uniform(keys[15], (D, E), jnp.float32, math.log(31129.6), math.log(124518.4))), 31129.6, 124518.4)
    gate_up_weight = normal_values(keys[16], (2, E, D, FF), D ** -0.5, 0.1875, ((2, 8), (3, 4)), jnp.float32)
    gate_up_moment = normal_values(keys[17], (2, E, D, FF), (0.56 * (TOKENS // (TOP * E)) ** 0.5), 20.0, ((2, 8), (3, 4)), jnp.float32)
    gate_up_second = jnp.clip(jnp.exp(math.log(166.4) - 1.3862944 * jax.random.uniform(keys[18], (2, E, D, FF), jnp.float32) ** shard_levels(keys[18], (2, E, D, FF), ((2, 8), (3, 4)), -0.2, 0.2)), 41.6, 166.4)
    down_weight = normal_values(keys[19], (E, FF, D), (FF // 16) ** -0.5, 1.0, ((1, 4), (2, 8)), jnp.float32)
    down_moment = normal_values(keys[20], (E, FF, D), (0.12 * (TOKENS // (TOP * E)) ** 0.5), 4.0, ((1, 4), (2, 8)), jnp.float32)
    down_second = jnp.clip(jnp.exp(math.log(7.04) - 1.3862944 * jax.random.uniform(keys[21], (E, FF, D), jnp.float32) ** shard_levels(keys[21], (E, FF, D), ((1, 4), (2, 8)), -0.2, 0.2)), 1.76, 7.04)
    norm_gains = jnp.clip(1.0 + 0.1 * jax.random.normal(keys[22], (2, D), jnp.float32), 0.5, 1.5)
    gains_moment = normal_values(keys[23], (2, D), (0.25 * TOKENS ** 0.5), 128.0, (), jnp.float32)
    gains_second = jnp.clip(jnp.exp(jax.random.uniform(keys[24], (2, D), jnp.float32, math.log(2048.0), math.log(8192.0))), 2048.0, 8192.0)
    return dict(stream=stream, cotangent=cotangent, lengths=lengths, routes=routes, query_weight=query_weight, query_moment=query_moment, query_second=query_second, key_value_weight=key_value_weight, key_value_moment=key_value_moment, key_value_second=key_value_second, output_weight=output_weight, output_moment=output_moment, output_second=output_second, router_weight=router_weight, router_moment=router_moment, router_second=router_second, gate_up_weight=gate_up_weight, gate_up_moment=gate_up_moment, gate_up_second=gate_up_second, down_weight=down_weight, down_moment=down_moment, down_second=down_second, norm_gains=norm_gains, gains_moment=gains_moment, gains_second=gains_second)


EPS = 1e-05
HIGH = lax.Precision.HIGHEST
BETA_ONE = 0.9
BETA_TWO = 0.95
WEIGHT_DECAY = 0.1

@jax.custom_vjp
def low(v):
    return lax.optimization_barrier(v.astype(jnp.bfloat16)).astype(jnp.float32)

@jax.custom_vjp
def low_back(v):
    return v

def low_keep(v):
    return (low(v), None)

def low_pass(kept, grad):
    return (grad,)

def back_keep(v):
    return (v, None)

def back_low(kept, grad):
    return (low(grad),)
low.defvjp(low_keep, low_pass)
low_back.defvjp(back_keep, back_low)

def positions(length_row, row_count):
    end_points = jnp.cumsum(length_row).astype(jnp.int32)
    start_points = (end_points - length_row).astype(jnp.int32)
    row_index = jnp.arange(row_count, dtype=jnp.int32)
    segment = lax.optimization_barrier(jnp.sum((row_index[:, None] >= end_points[None, :]).astype(jnp.int32), 1)).astype(jnp.int32)
    member = segment[:, None] == jnp.arange(length_row.shape[0], dtype=jnp.int32)[None, :]
    position = (row_index - lax.optimization_barrier(jnp.sum(jnp.where(member, start_points[None, :], 0), 1))).astype(jnp.int32)
    return (segment, position)

def rope_tables(position, half_size):
    frequency = 10000.0 ** (-jnp.arange(half_size, dtype=jnp.float32) / half_size)
    angles = position.astype(jnp.float32)[:, None] * frequency[None, :]
    return (jnp.cos(angles), jnp.sin(angles))

def rotate(vectors, cosine, sine_part):
    half_size = vectors.shape[-1] // 2
    first_half = vectors[..., :half_size]
    second_half = vectors[..., half_size:]
    cosine_rows = cosine[:, None, :]
    sine_rows = sine_part[:, None, :]
    return jnp.concatenate([first_half * cosine_rows - second_half * sine_rows, second_half * cosine_rows + first_half * sine_rows], -1)

def softmax_rows(scores):
    maximum = lax.optimization_barrier(jnp.max(scores, -1, keepdims=True))
    exp_scores = jnp.exp(scores - maximum)
    return exp_scores / lax.optimization_barrier(jnp.sum(exp_scores, -1, keepdims=True))

def rms_norm(vectors, gain_row):
    return vectors * lax.rsqrt(lax.optimization_barrier(jnp.mean(vectors * vectors, -1, keepdims=True)) + EPS) * gain_row

def route_slots(routes_group, row_count, experts, capacity):
    flat_experts = routes_group.reshape(-1).astype(jnp.int32)
    flat_hot = (flat_experts[:, None] == jnp.arange(experts, dtype=jnp.int32)[None, :]).astype(jnp.int32)
    earlier = (jnp.cumsum(flat_hot, 0) - flat_hot).astype(jnp.int32)
    slot_rank = lax.optimization_barrier(jnp.sum(earlier * flat_hot, 1)).astype(jnp.int32)
    flat_index = (flat_experts * capacity + slot_rank).astype(jnp.int32)
    top_count = routes_group.shape[1]
    token_index = (jnp.arange(row_count * top_count, dtype=jnp.int32) // top_count).astype(jnp.int32)
    slot_table = jnp.full((experts * capacity,), row_count, jnp.int32).at[flat_index].set(token_index)
    return (slot_table, flat_index)

def adam_update(weight, gradient, moment, second, step_rate, decay_rate):
    new_moment = BETA_ONE * moment + (1.0 - BETA_ONE) * gradient
    new_second = BETA_TWO * second + (1.0 - BETA_TWO) * gradient * gradient
    moment_hat = new_moment / (1.0 - BETA_ONE ** STEP)
    second_hat = new_second / (1.0 - BETA_TWO ** STEP)
    new_weight = weight - step_rate * (moment_hat / (jnp.sqrt(second_hat) + 1e-08) + decay_rate * weight)
    return (new_moment, new_second, new_weight)

def group_forward(weights, inputs, segment, position, slot_table, flat_index, routes_group):
    query_w, pair_w, output_w, router_w, gate_up_w, down_w, gain_rows = weights
    cosine, sine_part = rope_tables(position, HD // 2)
    share_count = H // KVH
    score_scale = HD ** (-0.5)
    normed_one = low(rms_norm(inputs, gain_rows[0]))
    query_raw = low_back(jnp.dot(normed_one, low(query_w), precision=HIGH)).reshape(TOK_DP, H, HD)
    pair_raw = low_back(jnp.einsum('td,cdf->ctf', normed_one, low(pair_w), precision=HIGH))
    queries = low(rotate(query_raw, cosine, sine_part)).reshape(TOK_DP, KVH, share_count, HD)
    key_rows = low(rotate(pair_raw[0].reshape(TOK_DP, KVH, HD), cosine, sine_part))
    value_rows = low(pair_raw[1].reshape(TOK_DP, KVH, HD))
    block_rows = min(512, TOK_DP)
    row_index = jnp.arange(TOK_DP, dtype=jnp.int32)

    def attend(row_start):
        query_block = lax.dynamic_slice_in_dim(queries, row_start, block_rows, 0)
        segment_block = lax.dynamic_slice_in_dim(segment, row_start, block_rows, 0)
        index_block = (row_start + jnp.arange(block_rows, dtype=jnp.int32)).astype(jnp.int32)
        scores = low_back(score_scale * jnp.einsum('qkgd,tkd->kgqt', query_block, key_rows, precision=HIGH))
        allowed = (segment_block[:, None] == segment[None, :]) & (row_index[None, :] <= index_block[:, None])
        scores = jnp.where(allowed, scores, -1e+30)
        probabilities = softmax_rows(scores)
        return jnp.einsum('kgqt,tkd->qkgd', low(probabilities), value_rows, precision=HIGH)
    block_starts = (jnp.arange(TOK_DP // block_rows, dtype=jnp.int32) * block_rows).astype(jnp.int32)
    attended = lax.map(jax.checkpoint(attend), block_starts)
    attended = low(low_back(attended.reshape(TOK_DP, H * HD)))
    hidden = inputs + low_back(jnp.dot(attended, low(output_w), precision=HIGH))
    normed_two = low(rms_norm(hidden, gain_rows[1]))
    logits = jnp.dot(normed_two, low(router_w), precision=HIGH)
    chosen = (routes_group[:, :, None] == jnp.arange(E, dtype=jnp.int32)[None, None, :]).astype(jnp.float32)
    gate_weights = softmax_rows(lax.optimization_barrier(jnp.sum(chosen * logits[:, None, :], -1)))
    padded = jnp.concatenate([normed_two, jnp.zeros((1, D), jnp.float32)], 0)
    slot_inputs = padded[slot_table].reshape(E, CAP, D)
    gate_up_low = low(gate_up_w)
    gate_pre = low_back(jnp.einsum('ecd,edf->ecf', slot_inputs, gate_up_low[0], precision=HIGH))
    up_pre = low_back(jnp.einsum('ecd,edf->ecf', slot_inputs, gate_up_low[1], precision=HIGH))
    middle = low(gate_pre * jax.nn.sigmoid(gate_pre) * up_pre)
    expert_out = low_back(jnp.einsum('ecf,efd->ecd', middle, low(down_w), precision=HIGH))
    routed = expert_out.reshape(E * CAP, D)[flat_index].reshape(TOK_DP, TOP, D)
    mixed = low_back(lax.optimization_barrier(jnp.sum(gate_weights[:, :, None] * routed, 1)))
    return hidden + mixed

def reference(stream, cotangent, lengths, routes, query_weight, query_moment, query_second, key_value_weight, key_value_moment, key_value_second, output_weight, output_moment, output_second, router_weight, router_moment, router_second, gate_up_weight, gate_up_moment, gate_up_second, down_weight, down_moment, down_second, norm_gains, gains_moment, gains_second):
    weights = (query_weight, key_value_weight, output_weight, router_weight, gate_up_weight, down_weight, norm_gains)

    def one_group(totals, group_args):
        inputs, back_rows, length_row, routes_group = group_args
        segment, position = positions(length_row, TOK_DP)
        slot_table, flat_index = route_slots(routes_group, TOK_DP, E, CAP)

        def forward(weight_tuple, inputs_inner):
            return group_forward(weight_tuple, inputs_inner, segment, position, slot_table, flat_index, routes_group)
        outcome, pullback = jax.vjp(forward, weights, inputs)
        weight_grads, input_grad = pullback(back_rows)
        totals = jax.tree.map(lambda summed, gradient: summed + gradient, totals, weight_grads)
        return (totals, (outcome, input_grad))
    zero_totals = jax.tree.map(jnp.zeros_like, weights)
    group_args = (stream.reshape(N_DP, TOK_DP, D), cotangent.reshape(N_DP, TOK_DP, D), lengths, routes.reshape(N_DP, TOK_DP, TOP))
    totals, (outcomes, input_grads) = lax.scan(one_group, zero_totals, group_args)
    query_grad, pair_grad, output_grad, router_grad, gate_up_grad, down_grad, gain_grad = totals
    rate_wide = 2.0 * D ** (-0.5)
    rate_output = 2.0 * max(1, 2 * H * HD // TOK_DP) ** (-0.5)
    rate_router = 2.0 * (4 * D) ** (-0.5)
    rate_down = 2.0 * (FF // 16) ** (-0.5)
    query_moment_new, query_second_new, query_weight_new = adam_update(query_weight, query_grad, query_moment, query_second, rate_wide, WEIGHT_DECAY)
    pair_moment_new, pair_second_new, pair_weight_new = adam_update(key_value_weight, pair_grad, key_value_moment, key_value_second, rate_wide, WEIGHT_DECAY)
    output_moment_new, output_second_new, output_weight_new = adam_update(output_weight, output_grad, output_moment, output_second, rate_output, WEIGHT_DECAY)
    router_moment_new, router_second_new, router_weight_new = adam_update(router_weight, router_grad, router_moment, router_second, rate_router, WEIGHT_DECAY)
    gate_up_moment_new, gate_up_second_new, gate_up_weight_new = adam_update(gate_up_weight, gate_up_grad, gate_up_moment, gate_up_second, rate_wide, WEIGHT_DECAY)
    down_moment_new, down_second_new, down_weight_new = adam_update(down_weight, down_grad, down_moment, down_second, rate_down, WEIGHT_DECAY)
    gains_moment_new, gains_second_new, gains_new = adam_update(norm_gains, gain_grad, gains_moment, gains_second, 0.2, 0.0)
    return (outcomes.reshape(TOKENS, D), input_grads.reshape(TOKENS, D), query_moment_new, query_second_new, query_weight_new, pair_moment_new, pair_second_new, pair_weight_new, output_moment_new, output_second_new, output_weight_new, router_moment_new, router_second_new, router_weight_new, gate_up_moment_new, gate_up_second_new, gate_up_weight_new, down_moment_new, down_second_new, down_weight_new, gains_moment_new, gains_second_new, gains_new)
```

```python
import jax
import jax.numpy as jnp
from jax import lax
from jax.experimental import pallas as pl
from jax.experimental.pallas import tpu as pltpu
from jax.sharding import Mesh
from jax.sharding import PartitionSpec as P

D = 1024
H = 16
HD = 64
FF = 512
STEP = 10


EPS = 1e-05
HIGH = lax.Precision.HIGHEST
BETA_ONE = 0.9
BETA_TWO = 0.95
WEIGHT_DECAY = 0.1
LANES = 128
BF = jnp.bfloat16
F32 = jnp.float32
Z, Y, X, C = 4, 2, 2, 2
EVERY = ("blk", "z", "y", "x", "core")
DATA = ("blk", "z", "y")


def positions(length_row, row_index):
    end_points = jnp.cumsum(length_row)
    start_points = end_points - length_row
    segment = jnp.sum((row_index[:, None] >= end_points[None, :]).astype(jnp.int32), 1)
    member = segment[:, None] == jnp.arange(length_row.shape[0], dtype=jnp.int32)[None, :]
    position = row_index - jnp.sum(jnp.where(member, start_points[None, :], 0), 1)
    return (segment, position)


def rope_tables(position, half_size):
    frequency = 10000.0 ** (-jnp.arange(half_size, dtype=jnp.float32) / half_size)
    angles = position.astype(jnp.float32)[:, None] * frequency[None, :]
    return (jnp.cos(angles), jnp.sin(angles))


def rotate(vectors, cosine, sine_part):
    half_size = vectors.shape[-1] // 2
    first_half = vectors[..., :half_size]
    second_half = vectors[..., half_size:]
    cosine_rows = cosine[:, None, :]
    sine_rows = sine_part[:, None, :]
    return jnp.concatenate(
        [
            first_half * cosine_rows - second_half * sine_rows,
            second_half * cosine_rows + first_half * sine_rows,
        ],
        -1,
    )


def adam_update(weight, gradient, moment, second, step_rate, decay_rate):
    new_moment = BETA_ONE * moment + (1.0 - BETA_ONE) * gradient
    new_second = BETA_TWO * second + (1.0 - BETA_TWO) * gradient * gradient
    moment_hat = new_moment / (1.0 - BETA_ONE**STEP)
    second_hat = new_second / (1.0 - BETA_TWO**STEP)
    new_weight = weight - step_rate * (
        moment_hat / (jnp.sqrt(second_hat) + 1e-08) + decay_rate * weight
    )
    return (new_moment, new_second, new_weight)


def partner(value, axis, mask=1):
    size = lax.axis_size(axis)
    return lax.ppermute(value, axis, [(i, i ^ mask) for i in range(size)])


def to_absolute(stacked, axis, dim):
    place = lax.axis_index(axis)
    bit = 1
    while bit < stacked.shape[dim]:
        order = [k ^ bit for k in range(stacked.shape[dim])]
        parts = [lax.slice_in_dim(stacked, k, k + 1, axis=dim) for k in order]
        other = jnp.concatenate(parts, dim)
        stacked = jnp.where((place & bit) != 0, other, stacked)
        bit *= 2
    return stacked


def pick(value, index, dim):
    return lax.dynamic_index_in_dim(value, index, dim, keepdims=False)


def gather_tensor(own):
    across = partner(own, "x")
    beside = partner(own, "core")
    return [own, beside, across, partner(across, "core")]


def scatter_tensor(blocks):
    sent = jnp.stack([blocks[1], blocks[3]]).astype(BF)
    got = partner(sent, "core").astype(F32)
    mine = blocks[0] + got[0]
    theirs = (blocks[2] + got[1]).astype(BF)
    return mine + partner(theirs, "x").astype(F32)


def nt_dot(left, right):
    return lax.dot_general(left, right, (((1,), (1,)), ((), ())), preferred_element_type=F32)


def expert_kernel(base, r0, r1, b0, b1, w, gu, gm, mixed, part, rows, back, acc_m, acc_p, acc_g):
    i = pl.program_id(0)
    half = r0.shape[0]

    @pl.when(i == 0)
    def _():
        rows[:half, :] = r0[...]
        rows[half:, :] = r1[...]
        back[:half, :] = b0[...]
        back[half:, :] = b1[...]
        acc_m[...] = jnp.zeros_like(acc_m)
        acc_p[...] = jnp.zeros_like(acc_p)
        acc_g[...] = jnp.zeros_like(acc_g)

    expert = base[0] + i
    mine = rows[:, :D]
    gate_lanes = rows[:, D:].astype(F32)
    lane = lax.broadcasted_iota(jnp.int32, gate_lanes.shape, 1)
    wanted = (lane == expert) | (lane == expert + 32)
    gate = jnp.sum(jnp.where(wanted, gate_lanes, 0.0), 1, keepdims=True)
    wg = w[0, :, :FF]
    wu = w[0, :, FF : 2 * FF]
    wd = w[0, :, 2 * FF :]
    gate_pre = jnp.dot(mine, wg, preferred_element_type=F32)
    up_pre = jnp.dot(mine, wu, preferred_element_type=F32)
    raw_back = jnp.dot(back[...], wd, preferred_element_type=F32)
    sig = jax.nn.sigmoid(gate_pre)
    active = gate_pre * sig
    middle = (active * up_pre).astype(BF).astype(F32)
    gate_grad = jnp.sum(middle * raw_back, 1, keepdims=True)
    acc_g[...] += jnp.where(lane == expert, gate_grad, 0.0)
    scaled = (gate * middle).astype(BF)
    middle_back = gate * raw_back
    gate_back = (middle_back * up_pre * sig * (1.0 + gate_pre * (1.0 - sig))).astype(BF)
    up_back = (middle_back * active).astype(BF)
    gu[:, :FF] = gate_back
    gu[:, FF:] = up_back
    gm[...] = scaled
    acc_m[...] += nt_dot(scaled, wd)
    acc_p[...] += nt_dot(gate_back, wg) + nt_dot(up_back, wu)

    @pl.when(i == pl.num_programs(0) - 1)
    def _():
        mixed[...] = acc_m[...].astype(BF)
        part[:, :D] = acc_p[...].astype(BF)
        part[:, D:] = acc_g[...].astype(BF)


def expert_chunk(base, r0, r1, b0, b1, weights):
    together = weights.shape[0]
    half, wide = r0.shape
    count = 2 * half
    whole = lambda i, s: (0, 0)
    return pl.pallas_call(
        expert_kernel,
        grid_spec=pltpu.PrefetchScalarGridSpec(
            num_scalar_prefetch=1,
            grid=(together,),
            in_specs=[
                pl.BlockSpec((half, wide), whole),
                pl.BlockSpec((half, wide), whole),
                pl.BlockSpec((half, D), whole),
                pl.BlockSpec((half, D), whole),
                pl.BlockSpec((1, D, 3 * FF), lambda i, s: (i, 0, 0)),
            ],
            out_specs=[
                pl.BlockSpec((count, 2 * FF), lambda i, s: (0, i)),
                pl.BlockSpec((count, FF), lambda i, s: (0, i)),
                pl.BlockSpec((count, D), whole),
                pl.BlockSpec((count, wide), whole),
            ],
            scratch_shapes=[
                pltpu.VMEM((count, wide), BF),
                pltpu.VMEM((count, D), BF),
                pltpu.VMEM((count, D), F32),
                pltpu.VMEM((count, D), F32),
                pltpu.VMEM((count, LANES), F32),
            ],
        ),
        out_shape=[
            jax.ShapeDtypeStruct((count, together * 2 * FF), BF),
            jax.ShapeDtypeStruct((count, together * FF), BF),
            jax.ShapeDtypeStruct((count, D), BF),
            jax.ShapeDtypeStruct((count, wide), BF),
        ],
        compiler_params=pltpu.CompilerParams(vmem_limit_bytes=48 * 1024 * 1024),
        cost_estimate=pl.CostEstimate(
            flops=12 * together * count * D * FF,
            bytes_accessed=6 * together * D * FF + 16 * count * D,
            transcendentals=together * count * FF,
        ),
        name="experts",
    )(base, r0, r1, b0, b1, weights)


def body(
    stream,
    cotangent,
    lengths,
    routes,
    query_weight,
    query_moment,
    query_second,
    key_value_weight,
    key_value_moment,
    key_value_second,
    output_weight,
    output_moment,
    output_second,
    router_weight,
    router_moment,
    router_second,
    gate_up_weight,
    gate_up_moment,
    gate_up_second,
    down_weight,
    down_moment,
    down_second,
    norm_gains,
    gains_moment,
    gains_second,
):
    blocks = lax.axis_size("blk")
    z, y, x, c = (lax.axis_index(a) for a in ("z", "y", "x", "core"))
    place = x * C + c
    local_rows = stream.shape[0]
    group_rows = local_rows * X * C
    experts = down_weight.shape[0]
    depth = query_weight.shape[0]
    deep = depth * blocks
    block_rows = min(512, group_rows)
    block_total = group_rows // block_rows
    query_wide = query_weight.shape[1]
    pair_wide = key_value_weight.shape[2]
    query_heads = query_wide // HD
    pair_heads = pair_wide // HD
    share_count = query_heads // pair_heads
    score_scale = HD ** (-0.5)
    together = experts // (Z * C)
    row_index = jnp.concatenate(
        [(place ^ b) * local_rows + jnp.arange(local_rows, dtype=jnp.int32) for b in range(X * C)]
    )
    segment, position = positions(lengths[0], row_index)
    cosine, sine_part = rope_tables(position, HD // 2)

    attn_own = jnp.concatenate(
        [query_weight, key_value_weight[0], key_value_weight[1], output_weight.T], 1
    ).astype(BF)
    if blocks > 1:
        attn_own = lax.all_gather(attn_own, "blk", axis=0, tiled=True)
    attn_z = jnp.stack([attn_own] + [partner(attn_own, "z", s) for s in range(1, Z)])
    attn_y = jnp.stack([attn_z, partner(attn_z, "y")], 1)
    attn_all = to_absolute(to_absolute(attn_y, "y", 1), "z", 0)
    attn_wide = attn_own.shape[1]
    if blocks > 1:
        attn_all = attn_all.reshape(Z, Y, blocks, depth, attn_wide).transpose(2, 0, 1, 3, 4)
    attn_all = attn_all.reshape(D, attn_wide)
    first_pair = query_wide + pair_wide
    second_pair = first_pair + pair_wide
    qkv_full = attn_all[:, :second_pair]
    output_full = attn_all[:, second_pair:]

    scale_one = lax.rsqrt(jnp.mean(stream * stream, -1, keepdims=True) + EPS)
    normed_one = (stream * scale_one * norm_gains[0]).astype(BF)
    rows_one = jnp.concatenate(gather_tensor(normed_one), 0)

    back_own = cotangent.astype(BF)
    back_z = [back_own] + [partner(back_own, "z", s) for s in range(1, Z)]
    back_pairs = [(v, partner(v, "core")) for v in back_z]

    expert_own = jnp.concatenate(
        [gate_up_weight[0], gate_up_weight[1], down_weight.transpose(0, 2, 1)], 2
    ).astype(BF)
    expert_wide = expert_own.shape[2]
    if blocks > 1:
        expert_own = lax.all_gather(expert_own, "blk", axis=1, tiled=True)
    expert_own = expert_own.reshape(Z, C, together, deep, expert_wide)
    kept = pick(expert_own, c, 1)
    moved = partner(pick(expert_own, 1 - c, 1), "core")
    both = jnp.stack([kept, moved])
    from_z = [pick(both, z, 1)] + [
        partner(pick(both, z ^ s, 1), "z", s) for s in range(1, Z)
    ]
    pieces = jnp.stack(from_z, 1)
    here = [[None, None], [None, None]]
    piece_a, piece_b = pieces[0], pieces[1]
    a_x = partner(piece_a, "x")
    b_y = partner(piece_b, "y")
    grid_a = jnp.stack(
        [jnp.stack([piece_a, a_x]), jnp.stack([partner(piece_a, "y"), partner(a_x, "y")])]
    )
    grid_b = jnp.stack(
        [jnp.stack([piece_b, partner(piece_b, "x")]), jnp.stack([b_y, partner(b_y, "x")])]
    )
    grid = jnp.stack([grid_a, grid_b], 3).reshape(
        Y, X, Z, C, together, blocks, depth, 3, expert_wide // 3
    )
    grid = to_absolute(to_absolute(grid, "y", 0), "z", 2)
    expert_weights = grid.transpose(4, 5, 2, 0, 6, 7, 1, 3, 8).reshape(together, D, 3 * FF)

    qkv_raw = jnp.dot(rows_one, qkv_full, preferred_element_type=F32)
    queries = (
        rotate(qkv_raw[:, :query_wide].reshape(group_rows, query_heads, HD), cosine, sine_part)
        .astype(BF)
        .reshape(group_rows, pair_heads, share_count, HD)
    )
    key_rows = rotate(
        qkv_raw[:, query_wide:first_pair].reshape(group_rows, pair_heads, HD), cosine, sine_part
    ).astype(BF)
    value_rows = qkv_raw[:, first_pair:].reshape(group_rows, pair_heads, HD).astype(BF)

    def block_scores(row_start):
        query_block = queries[row_start : row_start + block_rows]
        segment_block = segment[row_start : row_start + block_rows]
        index_block = row_index[row_start : row_start + block_rows]
        scores = score_scale * jnp.einsum(
            "qkgd,tkd->kgqt", query_block, key_rows, preferred_element_type=F32
        )
        allowed = (segment_block[:, None] == segment[None, :]) & (
            row_index[None, :] <= index_block[:, None]
        )
        return (jnp.where(allowed, scores, -1e30), query_block)

    log_totals = []
    attended_blocks = []
    for block_index in range(block_total):
        scores, query_block = block_scores(block_index * block_rows)
        maximum = jnp.max(scores, -1, keepdims=True)
        log_total = maximum + jnp.log(jnp.sum(jnp.exp(scores - maximum), -1, keepdims=True))
        probabilities = jnp.exp(scores - log_total)
        attended_blocks.append(
            jnp.einsum(
                "kgqt,tkd->qkgd",
                probabilities.astype(BF),
                value_rows,
                preferred_element_type=F32,
            )
        )
        log_totals.append(log_total)
    attended = jnp.concatenate(attended_blocks, 0).reshape(group_rows, query_heads * HD).astype(BF)
    attention_part = nt_dot(attended, output_full)
    hidden = stream + scatter_tensor(
        [attention_part[b * local_rows : (b + 1) * local_rows] for b in range(X * C)]
    )
    scale_two = lax.rsqrt(jnp.mean(hidden * hidden, -1, keepdims=True) + EPS)
    normed_two = (hidden * scale_two * norm_gains[1]).astype(BF)

    router_low = router_weight.astype(BF)
    logits = jnp.dot(normed_two, router_low, preferred_element_type=F32)
    routes_own = lax.dynamic_slice_in_dim(routes, place * local_rows, local_rows, 0)
    chosen = jnp.any(
        routes_own[:, :, None] == jnp.arange(experts, dtype=jnp.int32)[None, None, :], 1
    )
    masked = jnp.where(chosen, logits, -jnp.inf)
    raised = jnp.exp(masked - jnp.max(masked, -1, keepdims=True))
    gates = raised / jnp.sum(raised, -1, keepdims=True)
    gates_high = gates.astype(BF)
    gates_low = (gates - gates_high.astype(F32)).astype(BF)
    rows_own = jnp.concatenate(
        [
            normed_two,
            gates_high,
            gates_low,
            jnp.zeros((local_rows, LANES - 2 * experts), BF),
        ],
        1,
    )
    rows_z = [rows_own] + [partner(rows_own, "z", s) for s in range(1, Z)]
    rows_pairs = [(v, partner(v, "core")) for v in rows_z]
    base = ((z * C + c) * together).astype(jnp.int32).reshape(1)
    hidden_parts = []
    down_parts = []
    mixed_total = None
    back_total = None
    for s in range(Z):
        gu, gm, mixed, part = expert_chunk(base, *rows_pairs[s], *back_pairs[s], expert_weights)
        hidden_parts.append(gu)
        down_parts.append(gm)
        part_sum = part[:local_rows].astype(F32) + partner(part[local_rows:], "core").astype(F32)
        mixed_sum = mixed[:local_rows].astype(F32) + partner(mixed[local_rows:], "core").astype(F32)
        if s == 0:
            back_total, mixed_total = part_sum, mixed_sum
        else:
            back_total = back_total + partner(part_sum.astype(BF), "z", s).astype(F32)
            mixed_total = mixed_total + partner(mixed_sum.astype(BF), "z", s).astype(F32)
    result = hidden + mixed_total

    rows_all = jnp.concatenate([v[:, :D] for pair in rows_pairs for v in pair], 0)
    back_all = jnp.concatenate([v for pair in back_pairs for v in pair], 0)
    hidden_grad = lax.dot_general(
        rows_all,
        jnp.concatenate(hidden_parts, 0),
        (((0,), (0,)), ((), ())),
        preferred_element_type=F32,
    ).astype(BF)
    down_grad = lax.dot_general(
        back_all,
        jnp.concatenate(down_parts, 0),
        (((0,), (0,)), ((), ())),
        preferred_element_type=F32,
    ).astype(BF)
    lane_wide = expert_wide // 3
    grads = jnp.concatenate(
        [
            hidden_grad.reshape(blocks, Z, Y, depth, together, 2, X, C, lane_wide),
            down_grad.reshape(blocks, Z, Y, depth, together, 1, X, C, lane_wide),
        ],
        5,
    )
    grads = grads.transpose(7, 6, 2, 1, 4, 0, 3, 5, 8).reshape(
        C, X, Y, Z, together, deep, expert_wide
    )
    grads_a, grads_b = grads[0], grads[1]
    keep_a = pick(grads_a, y, 1).astype(F32)
    got_a = partner(pick(grads_a, 1 - y, 1), "y").astype(F32)
    sum_a = keep_a + got_a
    total_a = sum_a[0] + partner(sum_a[1].astype(BF), "x").astype(F32)
    sum_b = grads_b[0].astype(F32) + partner(grads_b[1], "x").astype(F32)
    total_b = pick(sum_b, y, 0) + partner(pick(sum_b, 1 - y, 0).astype(BF), "y").astype(F32)
    totals = jnp.stack([total_a, total_b]).astype(BF)
    owned_z = jnp.stack(
        [pick(totals, z, 1)] + [partner(pick(totals, z ^ s, 1), "z", s) for s in range(1, Z)], 1
    )
    owned = jnp.stack([owned_z[0], partner(owned_z[1], "core")], 1)
    owned = to_absolute(to_absolute(owned, "core", 1), "z", 0)
    owned = owned.reshape(experts, deep, expert_wide)
    if blocks > 1:
        owned = lax.psum_scatter(owned.astype(F32), "blk", scatter_dimension=1, tiled=True)
    owned = owned.reshape(experts, depth, 3, lane_wide).astype(F32)
    gate_up_grad = jnp.stack([owned[:, :, 0], owned[:, :, 1]])
    down_owned = owned[:, :, 2].transpose(0, 2, 1)

    expert_part = back_total[:, :D]
    gate_grad = back_total[:, D : D + experts]
    logit_back = gates * (gate_grad - jnp.sum(gates * gate_grad, -1, keepdims=True))
    router_part = jnp.dot(normed_two.astype(F32).T, logit_back, precision=HIGH)
    normed_two_back = expert_part + jnp.dot(logit_back, router_low.astype(F32).T, precision=HIGH)
    unit_two = hidden * scale_two
    weighted_two = normed_two_back * norm_gains[1]
    hidden_back = cotangent + scale_two * (
        weighted_two - unit_two * jnp.mean(weighted_two * unit_two, -1, keepdims=True)
    )
    gain_part_two = jnp.sum(normed_two_back * unit_two, 0)
    attention_back = jnp.concatenate(gather_tensor(hidden_back.astype(BF)), 0)
    output_grad = lax.dot_general(
        attention_back, attended, (((0,), (0,)), ((), ())), preferred_element_type=F32
    )
    attended_back = jnp.dot(attention_back, output_full, preferred_element_type=F32)
    attended_back = attended_back.astype(BF).reshape(group_rows, pair_heads, share_count, HD)
    key_grad = jnp.zeros((group_rows, pair_heads, HD), F32)
    value_grad = jnp.zeros((group_rows, pair_heads, HD), F32)
    query_blocks = []
    for block_index in range(block_total):
        row_start = block_index * block_rows
        scores, query_block = block_scores(row_start)
        probabilities = jnp.exp(scores - log_totals[block_index])
        back_block = attended_back[row_start : row_start + block_rows]
        prob_back = jnp.einsum(
            "qkgd,tkd->kgqt", back_block, value_rows, preferred_element_type=F32
        )
        inner_sum = jnp.sum(probabilities * prob_back, -1, keepdims=True)
        score_back = (probabilities * (prob_back - inner_sum)).astype(BF)
        query_blocks.append(
            score_scale
            * jnp.einsum("kgqt,tkd->qkgd", score_back, key_rows, preferred_element_type=F32)
        )
        key_grad = key_grad + score_scale * jnp.einsum(
            "kgqt,qkgd->tkd", score_back, query_block, preferred_element_type=F32
        )
        value_grad = value_grad + jnp.einsum(
            "kgqt,qkgd->tkd", probabilities.astype(BF), back_block, preferred_element_type=F32
        )
    query_grad_rows = jnp.concatenate(query_blocks, 0).reshape(group_rows, query_heads, HD)
    query_back = rotate(query_grad_rows, cosine, -sine_part).reshape(group_rows, query_wide)
    key_back = rotate(key_grad, cosine, -sine_part).reshape(group_rows, pair_wide)
    value_back = value_grad.reshape(group_rows, pair_wide)
    qkv_back = jnp.concatenate([query_back, key_back, value_back], 1).astype(BF)
    qkv_grad = lax.dot_general(
        rows_one, qkv_back, (((0,), (0,)), ((), ())), preferred_element_type=F32
    )
    normed_part = nt_dot(qkv_back, qkv_full)
    normed_one_back = scatter_tensor(
        [normed_part[b * local_rows : (b + 1) * local_rows] for b in range(X * C)]
    )
    unit_one = stream * scale_one
    weighted_one = normed_one_back * norm_gains[0]
    stream_grad = hidden_back + scale_one * (
        weighted_one - unit_one * jnp.mean(weighted_one * unit_one, -1, keepdims=True)
    )
    gain_one = jnp.sum(normed_one_back * unit_one, 0)

    def data_scatter(grad):
        wide = grad.shape[1]
        grad = grad.reshape(blocks, Z, Y, depth, wide).transpose(2, 1, 0, 3, 4)
        grad = grad.reshape(Y, Z, deep, wide)
        half = pick(grad, y, 0) + partner(pick(grad, 1 - y, 0).astype(BF), "y").astype(F32)
        total = pick(half, z, 0)
        for s in range(1, Z):
            total = total + partner(pick(half, z ^ s, 0).astype(BF), "z", s).astype(F32)
        if blocks > 1:
            total = lax.psum_scatter(total, "blk", scatter_dimension=0, tiled=True)
        return total

    output_owned = data_scatter(output_grad).T
    qkv_owned = data_scatter(qkv_grad)
    query_owned = qkv_owned[:, :query_wide]
    pair_owned = jnp.stack([qkv_owned[:, query_wide:first_pair], qkv_owned[:, first_pair:]])
    gain_two, router_grad = lax.psum((gain_part_two, router_part), EVERY)
    for axis, mask in (("core", 1), ("x", 1), ("y", 1), ("z", 1), ("z", 2)):
        gain_one = gain_one + partner(gain_one, axis, mask)
    if blocks > 1:
        gain_one = lax.psum(gain_one, "blk")
    gain_grad = jnp.stack([gain_one, gain_two])
    rate_wide = 2.0 * D ** (-0.5)
    rate_output = 2.0 * max(1, 2 * H * HD // group_rows) ** (-0.5)
    rate_router = 2.0 * (4 * D) ** (-0.5)
    rate_down = 2.0 * (FF // 16) ** (-0.5)
    query_new = adam_update(
        query_weight, query_owned, query_moment, query_second, rate_wide, WEIGHT_DECAY
    )
    pair_new = adam_update(
        key_value_weight, pair_owned, key_value_moment, key_value_second, rate_wide, WEIGHT_DECAY
    )
    output_new = adam_update(
        output_weight, output_owned, output_moment, output_second, rate_output, WEIGHT_DECAY
    )
    router_new = adam_update(
        router_weight, router_grad, router_moment, router_second, rate_router, WEIGHT_DECAY
    )
    gate_up_new = adam_update(
        gate_up_weight, gate_up_grad, gate_up_moment, gate_up_second, rate_wide, WEIGHT_DECAY
    )
    down_new = adam_update(
        down_weight, down_owned, down_moment, down_second, rate_down, WEIGHT_DECAY
    )
    gains_new = adam_update(norm_gains, gain_grad, gains_moment, gains_second, 0.2, 0.0)
    return (
        (result, stream_grad)
        + query_new
        + pair_new
        + output_new
        + router_new
        + gate_up_new
        + down_new
        + gains_new
    )


def solution(mesh):
    data_size, tensor_size = mesh.shape["dp"], mesh.shape["tensor"]
    blocks = data_size // (Z * Y)
    fine = Mesh(mesh.devices.reshape(blocks, Z, Y, tensor_size // C, C), EVERY)
    split = ("x", "core")
    rows = P(EVERY, None)
    wide = P(DATA, split)
    pair = P(None, DATA, split)
    tall = P(split, DATA)
    gate_up = P(None, None, DATA, split)
    down = P(None, split, DATA)
    group = P(DATA, None)
    return jax.shard_map(
        body,
        mesh=fine,
        in_specs=(rows, rows, group, group)
        + (wide,) * 3
        + (pair,) * 3
        + (tall,) * 3
        + (P(),) * 3
        + (gate_up,) * 3
        + (down,) * 3
        + (P(),) * 3,
        out_specs=(rows, rows)
        + (wide,) * 3
        + (pair,) * 3
        + (tall,) * 3
        + (P(),) * 3
        + (gate_up,) * 3
        + (down,) * 3
        + (P(),) * 3,
        check_vma=False,
    )
```

```python
import jax
import jax.numpy as jnp
from jax import lax
from jax.experimental import pallas as pl
from jax.experimental.pallas import tpu as pltpu
from jax.sharding import Mesh
from jax.sharding import PartitionSpec as P

D = 1024
H = 16
HD = 64
FF = 512
STEP = 10


EPS = 1e-05
HIGH = lax.Precision.HIGHEST
BETA_ONE = 0.9
BETA_TWO = 0.95
WEIGHT_DECAY = 0.1
LANES = 128
BF = jnp.bfloat16
F32 = jnp.float32
Z, Y, X, C = 4, 2, 2, 2
EVERY = ("blk", "z", "y", "x", "core")
DATA = ("blk", "z", "y")


def positions(length_row, row_index):
    end_points = jnp.cumsum(length_row)
    start_points = end_points - length_row
    segment = jnp.sum((row_index[:, None] >= end_points[None, :]).astype(jnp.int32), 1)
    member = segment[:, None] == jnp.arange(length_row.shape[0], dtype=jnp.int32)[None, :]
    position = row_index - jnp.sum(jnp.where(member, start_points[None, :], 0), 1)
    return (segment, position)


def rope_tables(position, half_size):
    frequency = 10000.0 ** (-jnp.arange(half_size, dtype=jnp.float32) / half_size)
    angles = position.astype(jnp.float32)[:, None] * frequency[None, :]
    return (jnp.cos(angles), jnp.sin(angles))


def rotate(vectors, cosine, sine_part):
    half_size = vectors.shape[-1] // 2
    first_half = vectors[..., :half_size]
    second_half = vectors[..., half_size:]
    cosine_rows = cosine[:, None, :]
    sine_rows = sine_part[:, None, :]
    return jnp.concatenate(
        [
            first_half * cosine_rows - second_half * sine_rows,
            second_half * cosine_rows + first_half * sine_rows,
        ],
        -1,
    )


def adam_update(weight, gradient, moment, second, step_rate, decay_rate):
    new_moment = BETA_ONE * moment + (1.0 - BETA_ONE) * gradient
    new_second = BETA_TWO * second + (1.0 - BETA_TWO) * gradient * gradient
    moment_hat = new_moment / (1.0 - BETA_ONE**STEP)
    second_hat = new_second / (1.0 - BETA_TWO**STEP)
    new_weight = weight - step_rate * (
        moment_hat / (jnp.sqrt(second_hat) + 1e-08) + decay_rate * weight
    )
    return (new_moment, new_second, new_weight)


def partner(value, axis, mask=1):
    size = lax.axis_size(axis)
    return lax.ppermute(value, axis, [(i, i ^ mask) for i in range(size)])


def to_absolute(stacked, axis, dim):
    place = lax.axis_index(axis)
    bit = 1
    while bit < stacked.shape[dim]:
        order = [k ^ bit for k in range(stacked.shape[dim])]
        parts = [lax.slice_in_dim(stacked, k, k + 1, axis=dim) for k in order]
        other = jnp.concatenate(parts, dim)
        stacked = jnp.where((place & bit) != 0, other, stacked)
        bit *= 2
    return stacked


def pick(value, index, dim):
    return lax.dynamic_index_in_dim(value, index, dim, keepdims=False)


def total_sum(value):
    for axis, mask in (("core", 1), ("x", 1), ("y", 1), ("z", 1), ("z", 2)):
        value = value + partner(value, axis, mask)
    if lax.axis_size("blk") > 1:
        value = lax.psum(value, "blk")
    return value


def gather_tensor(own):
    across = partner(own, "x")
    beside = partner(own, "core")
    return [own, beside, across, partner(across, "core")]


def scatter_tensor(blocks):
    sent = jnp.stack([blocks[1], blocks[3]]).astype(BF)
    got = partner(sent, "core").astype(F32)
    mine = blocks[0] + got[0]
    theirs = (blocks[2] + got[1]).astype(BF)
    return mine + partner(theirs, "x").astype(F32)


def nt_dot(left, right):
    return lax.dot_general(left, right, (((1,), (1,)), ((), ())), preferred_element_type=F32)


def tn_dot(left, right):
    return lax.dot_general(left, right, (((0,), (0,)), ((), ())), preferred_element_type=F32)


def spec(shape, index):
    return pl.BlockSpec(shape, index)


def assemble_kernel(offsets, *refs):
    pieces, (wgu, wd) = refs[:8], refs[8:]
    for k, piece in enumerate(pieces):
        across, beside, far = k // 4, k // 2 % 2, k % 2
        hidden = (beside * C + far) * LANES
        for s in range(Z):
            row = pl.multiple_of(offsets[s * Y + across], LANES)
            wgu[0, pl.ds(row, LANES), hidden : hidden + LANES] = piece[s, 0, :LANES]
            wgu[0, pl.ds(row, LANES), FF + hidden : FF + hidden + LANES] = piece[
                s, 0, LANES : 2 * LANES
            ]
            wd[0, hidden : hidden + LANES, pl.ds(row, LANES)] = piece[s, 0, 2 * LANES :]


def assemble(offsets, pieces):
    count = pieces[0].shape[1]
    return pl.pallas_call(
        assemble_kernel,
        grid_spec=pltpu.PrefetchScalarGridSpec(
            num_scalar_prefetch=1,
            grid=(count,),
            in_specs=[spec((Z, 1, 3 * LANES, LANES), lambda i, o: (0, i, 0, 0))] * 8,
            out_specs=[
                spec((1, D, 2 * FF), lambda i, o: (i, 0, 0)),
                spec((1, FF, D), lambda i, o: (i, 0, 0)),
            ],
        ),
        out_shape=[
            jax.ShapeDtypeStruct((count, D, 2 * FF), BF),
            jax.ShapeDtypeStruct((count, FF, D), BF),
        ],
        compiler_params=pltpu.CompilerParams(vmem_limit_bytes=32 * 1024 * 1024),
        cost_estimate=pl.CostEstimate(
            flops=0, bytes_accessed=12 * count * D * FF, transcendentals=0
        ),
        name="assemble",
    )(offsets, *pieces)


def expert_kernel(first, chunk, half, experts, base, *refs):
    if first:
        r0, r1, b0, b1, wgu, wd = refs[:6]
        refs = refs[6:] if chunk == 0 else refs[10:]
        gu, gm, rows, back, mixed_out, part_out, acc_m, acc_p, acc_g = refs
    else:
        rows, back, wgu, wd, mixed_in, part_in = refs[:6]
        refs = refs[6:] if chunk == 0 else refs[8:]
        gu, gm, m0, m1, p0, p1, acc_m, acc_p, acc_g = refs
    i = pl.program_id(0)

    @pl.when(i == 0)
    def _():
        if first:
            rows[:half, :] = r0[...]
            rows[half:, :] = r1[...]
            back[:half, :] = b0[...]
            back[half:, :] = b1[...]
            acc_m[...] = jnp.zeros_like(acc_m)
            acc_p[...] = jnp.zeros_like(acc_p)
            acc_g[...] = jnp.zeros_like(acc_g)
        else:
            acc_m[...] = mixed_in[...]
            acc_p[...] = part_in[:, :D]
            acc_g[...] = part_in[:, D:]

    expert = base[0] + i
    wg = wgu[0, :, :FF]
    wu = wgu[0, :, FF:]
    wdown = wd[0]
    for t in range(2):
        here = slice(t * half, (t + 1) * half)
        mine = rows[here, :D]
        gate_lanes = rows[here, D:].astype(F32)
        lane = lax.broadcasted_iota(jnp.int32, gate_lanes.shape, 1)
        wanted = (lane == expert) | (lane == expert + experts)
        gate = jnp.sum(jnp.where(wanted, gate_lanes, 0.0), 1, keepdims=True)
        gate_pre = jnp.dot(mine, wg, preferred_element_type=F32)
        up_pre = jnp.dot(mine, wu, preferred_element_type=F32)
        raw_back = nt_dot(back[here, :], wdown)
        sig = jax.nn.sigmoid(gate_pre)
        active = gate_pre * sig
        middle = (active * up_pre).astype(BF).astype(F32)
        gate_grad = jnp.sum(middle * raw_back, 1, keepdims=True)
        acc_g[here, :] += jnp.where(lane == expert, gate_grad, 0.0)
        scaled = (gate * middle).astype(BF)
        middle_back = gate * raw_back
        gate_back = (middle_back * up_pre * (sig + active * (1.0 - sig))).astype(BF)
        up_back = (middle_back * active).astype(BF)
        gu[here, :FF] = gate_back
        gu[here, FF:] = up_back
        gm[here, :] = scaled
        acc_m[here, :] += jnp.dot(scaled, wdown, preferred_element_type=F32)
        acc_p[here, :] += nt_dot(gate_back, wg) + nt_dot(up_back, wu)

    @pl.when(i == pl.num_programs(0) - 1)
    def _():
        if first:
            mixed_out[...] = acc_m[...]
            part_out[:, :D] = acc_p[...]
            part_out[:, D:] = acc_g[...]
        else:
            m0[...] = acc_m[:half, :].astype(BF)
            m1[...] = acc_m[half:, :].astype(BF)
            p0[:, :D] = acc_p[:half, :].astype(BF)
            p0[:, D:] = acc_g[:half, :].astype(BF)
            p1[:, :D] = acc_p[half:, :].astype(BF)
            p1[:, D:] = acc_g[half:, :].astype(BF)


def expert_chunk(first, chunk, half, experts, base, tokens, weights, carried, sums):
    wgu, wd = weights
    together = wgu.shape[0]
    count = 2 * half
    wide = D + LANES
    whole = lambda i, s: (0, 0)
    at_chunk = lambda i, s: (chunk, 0)
    at_both = lambda i, s: (chunk, i)
    weight_specs = [
        spec((1, D, 2 * FF), lambda i, s: (i, 0, 0)),
        spec((1, FF, D), lambda i, s: (i, 0, 0)),
    ]
    any_spec = pl.BlockSpec(memory_space=pl.ANY)
    shape = jax.ShapeDtypeStruct
    hidden_specs = [spec((count, 2 * FF), at_both), spec((count, FF), at_both)]
    hidden_shapes = [
        shape((Z * count, together * 2 * FF), BF),
        shape((Z * count, together * FF), BF),
    ]
    if first:
        in_specs = [spec((half, wide), whole)] * 2 + [spec((half, D), whole)] * 2 + weight_specs
        operands = list(tokens) + [wgu, wd]
        out_specs = hidden_specs + [
            spec((count, wide), at_chunk),
            spec((count, D), at_chunk),
            spec((count, D), whole),
            spec((count, wide), whole),
        ]
        out_shape = hidden_shapes + [
            shape((Z * count, wide), BF),
            shape((Z * count, D), BF),
            shape((count, D), F32),
            shape((count, wide), F32),
        ]
    else:
        in_specs = (
            [spec((count, wide), at_chunk), spec((count, D), at_chunk)]
            + weight_specs
            + [spec((count, D), whole), spec((count, wide), whole)]
        )
        operands = list(tokens) + [wgu, wd] + list(sums)
        out_specs = hidden_specs + [spec((half, D), whole)] * 2 + [spec((half, wide), whole)] * 2
        out_shape = hidden_shapes + [shape((half, D), BF)] * 2 + [shape((half, wide), BF)] * 2
    aliases = {}
    if chunk > 0:
        aliases = {1 + len(operands) + k: k for k in range(len(carried))}
        in_specs = in_specs + [any_spec] * len(carried)
        operands = operands + list(carried)
    return pl.pallas_call(
        lambda *refs: expert_kernel(first, chunk, half, experts, *refs),
        grid_spec=pltpu.PrefetchScalarGridSpec(
            num_scalar_prefetch=1,
            grid=(together,),
            in_specs=in_specs,
            out_specs=out_specs,
            scratch_shapes=[
                pltpu.VMEM((count, D), F32),
                pltpu.VMEM((count, D), F32),
                pltpu.VMEM((count, LANES), F32),
            ],
        ),
        out_shape=out_shape,
        input_output_aliases=aliases,
        compiler_params=pltpu.CompilerParams(vmem_limit_bytes=48 * 1024 * 1024),
        cost_estimate=pl.CostEstimate(
            flops=12 * together * count * D * FF,
            bytes_accessed=6 * together * D * FF + 16 * count * D,
            transcendentals=together * count * FF,
        ),
        name="experts",
    )(base, *operands)


def grad_kernel(offsets, rows, back, gu, gm, keep_a, send_a, keep_b, send_b, hidden, down):
    hidden[...] = tn_dot(rows[:, :D], gu[...]).astype(BF)
    down[...] = tn_dot(gm[...], back[...]).astype(BF)
    for s in range(Z):
        for across in range(Y):
            row = pl.multiple_of(offsets[s * Y + across], LANES)
            for beside in range(X):
                for far in range(C):
                    at = (beside * C + far) * LANES
                    if far == 0:
                        target = (keep_a, send_a)[across].at[s, beside, 0]
                    else:
                        target = (keep_b, send_b)[beside].at[s, across, 0]
                    target[:LANES, :] = hidden[pl.ds(row, LANES), at : at + LANES]
                    target[LANES : 2 * LANES, :] = hidden[
                        pl.ds(row, LANES), FF + at : FF + at + LANES
                    ]
                    target[2 * LANES :, :] = down[at : at + LANES, pl.ds(row, LANES)]


def expert_grads(offsets, rows, back, gu, gm):
    count = rows.shape[0]
    together = gm.shape[1] // FF
    piece = spec((Z, 2, 1, 3 * LANES, LANES), lambda i, o: (0, 0, i, 0, 0))
    whole = lambda i, o: (0, 0)
    return pl.pallas_call(
        grad_kernel,
        grid_spec=pltpu.PrefetchScalarGridSpec(
            num_scalar_prefetch=1,
            grid=(together,),
            in_specs=[
                spec((count, D + LANES), whole),
                spec((count, D), whole),
                spec((count, 2 * FF), lambda i, o: (0, i)),
                spec((count, FF), lambda i, o: (0, i)),
            ],
            out_specs=[piece] * 4,
            scratch_shapes=[pltpu.VMEM((D, 2 * FF), BF), pltpu.VMEM((FF, D), BF)],
        ),
        out_shape=[jax.ShapeDtypeStruct((Z, 2, together, 3 * LANES, LANES), BF)] * 4,
        compiler_params=pltpu.CompilerParams(vmem_limit_bytes=56 * 1024 * 1024),
        cost_estimate=pl.CostEstimate(
            flops=6 * together * count * D * FF,
            bytes_accessed=4 * count * D + 12 * together * D * FF,
            transcendentals=0,
        ),
        name="expert_grads",
    )(offsets, rows, back, gu, gm)


def adam_kernel(rate_wide, rate_down, table, grad, *refs):
    ins, outs = refs[:6], refs[6:]
    for k in range(2):
        new = adam_update(
            ins[0][k],
            grad[0, 0, :, k * LANES : (k + 1) * LANES, :].astype(F32),
            ins[1][k],
            ins[2][k],
            rate_wide,
            WEIGHT_DECAY,
        )
        for ref, value in zip(outs[:3], new):
            ref[k] = value
    new = adam_update(
        ins[3][...],
        grad[0, 0, :, 2 * LANES :, :].astype(F32),
        ins[4][...],
        ins[5][...],
        rate_down,
        WEIGHT_DECAY,
    )
    for ref, value in zip(outs[3:], new):
        ref[...] = value


def expert_adam(table, grads, gate_up, down, rate_wide, rate_down):
    together = grads.shape[2]
    two = spec((2, together, LANES, LANES), lambda g, t: (0, g, 0, 0))
    one = spec((together, LANES, LANES), lambda g, t: (g, 0, 0))
    return pl.pallas_call(
        lambda *refs: adam_kernel(rate_wide, rate_down, *refs),
        grid_spec=pltpu.PrefetchScalarGridSpec(
            num_scalar_prefetch=1,
            grid=(Z * C,),
            in_specs=[
                spec(
                    (1, 1, together, 3 * LANES, LANES),
                    lambda g, t: (t[2 * g], t[2 * g + 1], 0, 0, 0),
                )
            ]
            + [two] * 3
            + [one] * 3,
            out_specs=[two] * 3 + [one] * 3,
        ),
        out_shape=[jax.ShapeDtypeStruct(v.shape, F32) for v in gate_up + down],
        compiler_params=pltpu.CompilerParams(vmem_limit_bytes=40 * 1024 * 1024),
        cost_estimate=pl.CostEstimate(
            flops=20 * 3 * grads.size,
            bytes_accessed=26 * grads.size,
            transcendentals=grads.size,
        ),
        name="expert_adam",
    )(table, grads, *gate_up, *down)


def body(
    stream,
    cotangent,
    lengths,
    routes,
    query_weight,
    query_moment,
    query_second,
    key_value_weight,
    key_value_moment,
    key_value_second,
    output_weight,
    output_moment,
    output_second,
    router_weight,
    router_moment,
    router_second,
    gate_up_weight,
    gate_up_moment,
    gate_up_second,
    down_weight,
    down_moment,
    down_second,
    norm_gains,
    gains_moment,
    gains_second,
):
    blocks = lax.axis_size("blk")
    z, y, x, c = (lax.axis_index(a) for a in ("z", "y", "x", "core"))
    place = x * C + c
    local_rows = stream.shape[0]
    group_rows = local_rows * X * C
    experts = down_weight.shape[0]
    depth = query_weight.shape[0]
    deep = depth * blocks
    block_rows = min(512, group_rows)
    block_total = group_rows // block_rows
    query_wide = query_weight.shape[1]
    pair_wide = key_value_weight.shape[2]
    query_heads = query_wide // HD
    pair_heads = pair_wide // HD
    share_count = query_heads // pair_heads
    score_scale = HD ** (-0.5)
    together = experts // (Z * C)
    row_index = jnp.concatenate(
        [(place ^ b) * local_rows + jnp.arange(local_rows, dtype=jnp.int32) for b in range(X * C)]
    )
    segment, position = positions(lengths[0], row_index)
    cosine, sine_part = rope_tables(position, HD // 2)

    attn_own = jnp.concatenate(
        [query_weight, key_value_weight[0], key_value_weight[1], output_weight.T], 1
    ).astype(BF)
    if blocks > 1:
        attn_own = lax.all_gather(attn_own, "blk", axis=0, tiled=True)
    attn_z = jnp.stack([attn_own] + [partner(attn_own, "z", s) for s in range(1, Z)])
    attn_y = jnp.stack([attn_z, partner(attn_z, "y")], 1)
    attn_all = to_absolute(to_absolute(attn_y, "y", 1), "z", 0)
    attn_wide = attn_own.shape[1]
    if blocks > 1:
        attn_all = attn_all.reshape(Z, Y, blocks, depth, attn_wide).transpose(2, 0, 1, 3, 4)
    attn_all = attn_all.reshape(D, attn_wide)
    first_pair = query_wide + pair_wide
    second_pair = first_pair + pair_wide
    qkv_full = attn_all[:, :second_pair]
    output_full = attn_all[:, second_pair:]

    scale_one = lax.rsqrt(jnp.mean(stream * stream, -1, keepdims=True) + EPS)
    normed_one = (stream * scale_one * norm_gains[0]).astype(BF)
    rows_one = jnp.concatenate(gather_tensor(normed_one), 0)

    back_own = cotangent.astype(BF)
    back_z = [back_own] + [partner(back_own, "z", s) for s in range(1, Z)]
    back_pairs = [(v, partner(v, "core")) for v in back_z]

    gate_up_low, down_low = gate_up_weight.astype(BF), down_weight.astype(BF)
    if blocks > 1:
        gate_up_low = lax.all_gather(gate_up_low, "blk", axis=2, tiled=True)
        down_low = lax.all_gather(down_low, "blk", axis=2, tiled=True)
    expert_own = jnp.concatenate([gate_up_low[0], gate_up_low[1], down_low], 1)
    expert_own = expert_own.reshape(Z, C, together, 3 * LANES, LANES)
    kept = pick(expert_own, c, 1)
    moved = partner(pick(expert_own, 1 - c, 1), "core")
    offsets = jnp.stack(
        [((z ^ s) * Y + (y ^ k)) * LANES for s in range(Z) for k in range(Y)]
    ).astype(jnp.int32)
    halves = 2
    per_half = together // halves
    half_weights = []
    for h in range(halves):
        span = slice(h * per_half, (h + 1) * per_half)
        near = [pick(kept[:, span], z, 0)]
        far = [pick(moved[:, span], z, 0)]
        for s in range(1, Z):
            got = partner(
                jnp.stack([pick(kept[:, span], z ^ s, 0), pick(moved[:, span], z ^ s, 0)]), "z", s
            )
            near.append(got[0])
            far.append(got[1])
        near, far = jnp.stack(near), jnp.stack(far)
        near_x = partner(near, "x")
        far_y = partner(far, "y")
        pieces = [
            near,
            far,
            near_x,
            partner(far, "x"),
            partner(near, "y"),
            far_y,
            partner(near_x, "y"),
            partner(far_y, "x"),
        ]
        wgu, wd = assemble(offsets, pieces)
        if blocks > 1:
            wgu = wgu.reshape(per_half, Z * Y, blocks, depth, 2 * FF)
            wgu = wgu.transpose(0, 2, 1, 3, 4).reshape(per_half, D, 2 * FF)
            wd = wd.reshape(per_half, FF, Z * Y, blocks, depth)
            wd = wd.transpose(0, 1, 3, 2, 4).reshape(per_half, FF, D)
        half_weights.append((wgu, wd))

    qkv_raw = jnp.dot(rows_one, qkv_full, preferred_element_type=F32)
    queries = (
        rotate(qkv_raw[:, :query_wide].reshape(group_rows, query_heads, HD), cosine, sine_part)
        .astype(BF)
        .reshape(group_rows, pair_heads, share_count, HD)
    )
    key_rows = rotate(
        qkv_raw[:, query_wide:first_pair].reshape(group_rows, pair_heads, HD), cosine, sine_part
    ).astype(BF)
    value_rows = qkv_raw[:, first_pair:].reshape(group_rows, pair_heads, HD).astype(BF)

    def block_scores(row_start):
        query_block = queries[row_start : row_start + block_rows]
        segment_block = segment[row_start : row_start + block_rows]
        index_block = row_index[row_start : row_start + block_rows]
        scores = score_scale * jnp.einsum(
            "qkgd,tkd->kgqt", query_block, key_rows, preferred_element_type=F32
        )
        allowed = (segment_block[:, None] == segment[None, :]) & (
            row_index[None, :] <= index_block[:, None]
        )
        return (jnp.where(allowed, scores, -1e30), query_block)

    log_totals = []
    attended_blocks = []
    for block_index in range(block_total):
        scores, query_block = block_scores(block_index * block_rows)
        maximum = jnp.max(scores, -1, keepdims=True)
        log_total = maximum + jnp.log(jnp.sum(jnp.exp(scores - maximum), -1, keepdims=True))
        probabilities = jnp.exp(scores - log_total)
        attended_blocks.append(
            jnp.einsum(
                "kgqt,tkd->qkgd",
                probabilities.astype(BF),
                value_rows,
                preferred_element_type=F32,
            )
        )
        log_totals.append(log_total)
    attended = jnp.concatenate(attended_blocks, 0).reshape(group_rows, query_heads * HD).astype(BF)
    attention_part = nt_dot(attended, output_full)
    hidden = stream + scatter_tensor(
        [attention_part[b * local_rows : (b + 1) * local_rows] for b in range(X * C)]
    )
    scale_two = lax.rsqrt(jnp.mean(hidden * hidden, -1, keepdims=True) + EPS)
    normed_two = (hidden * scale_two * norm_gains[1]).astype(BF)

    router_low = router_weight.astype(BF)
    logits = jnp.dot(normed_two, router_low, preferred_element_type=F32)
    routes_own = lax.dynamic_slice_in_dim(routes, place * local_rows, local_rows, 0)
    chosen = jnp.any(
        routes_own[:, :, None] == jnp.arange(experts, dtype=jnp.int32)[None, None, :], 1
    )
    masked = jnp.where(chosen, logits, -jnp.inf)
    raised = jnp.exp(masked - jnp.max(masked, -1, keepdims=True))
    gates = raised / jnp.sum(raised, -1, keepdims=True)
    gates_high = gates.astype(BF)
    gates_low = (gates - gates_high.astype(F32)).astype(BF)
    rows_own = jnp.concatenate(
        [
            normed_two,
            gates_high,
            gates_low,
            jnp.zeros((local_rows, LANES - 2 * experts), BF),
        ],
        1,
    )
    rows_z = [rows_own] + [partner(rows_own, "z", s) for s in range(1, Z)]
    rows_pairs = [(v, partner(v, "core")) for v in rows_z]
    base = ((z * C + c) * together).astype(jnp.int32).reshape(1)
    sums = []
    carried = ()
    for s in range(Z):
        out = expert_chunk(
            True,
            s,
            local_rows,
            experts,
            base,
            rows_pairs[s] + back_pairs[s],
            half_weights[0],
            carried,
            None,
        )
        carried = out[:4]
        sums.append(out[4:])
    rows_all, back_all = carried[2:]

    def to_pieces(rows):
        if blocks == 1:
            return rows
        own = rows[:, :D].reshape(-1, blocks, Z * Y, depth).transpose(0, 2, 1, 3)
        return jnp.concatenate([own.reshape(-1, D), rows[:, D:]], 1)

    def expert_sums(gu, gm):
        keep_a, send_a, keep_b, send_b = expert_grads(
            offsets, to_pieces(rows_all), to_pieces(back_all), gu, gm
        )
        sum_a = (keep_a.astype(F32) + partner(send_a, "y").astype(F32)).astype(BF)
        sum_b = (keep_b.astype(F32) + partner(send_b, "x").astype(F32)).astype(BF)
        total_a = sum_a[:, 0].astype(F32) + partner(sum_a[:, 1], "x").astype(F32)
        total_b = sum_b[:, 0].astype(F32) + partner(sum_b[:, 1], "y").astype(F32)
        total = jnp.stack([total_a, total_b], 1).astype(BF)
        owned = jnp.stack([total[0]] + [partner(total[s], "z", s) for s in range(1, Z)])
        return owned[:, 0], partner(owned[:, 1], "core")

    owned = [expert_sums(*carried[:2])]
    carried = ()
    back_total, mixed_parts = None, []
    for s in range(Z):
        out = expert_chunk(
            False,
            s,
            local_rows,
            experts,
            base + per_half,
            (rows_all, back_all),
            half_weights[1],
            carried,
            sums[s],
        )
        carried = out[:2]
        m0, m1, p0, p1 = out[2:]
        part_sum = p0.astype(F32) + partner(p1, "core").astype(F32)
        mixed_parts.append((m0, m1))
        if s == 0:
            back_total = part_sum
        else:
            back_total = back_total + partner(part_sum.astype(BF), "z", s).astype(F32)
    owned.append(expert_sums(*carried))
    mixed_total = None
    for s in range(Z):
        m0, m1 = mixed_parts[s]
        mixed_sum = m0.astype(F32) + partner(m1, "core").astype(F32)
        if s == 0:
            mixed_total = mixed_sum
        else:
            mixed_total = mixed_total + partner(mixed_sum.astype(BF), "z", s).astype(F32)
    result = hidden + mixed_total
    owned = jnp.stack([jnp.concatenate([h[k] for h in owned], 1) for k in range(C)])

    expert_part = back_total[:, :D]
    gate_grad = back_total[:, D : D + experts]
    logit_back = gates * (gate_grad - jnp.sum(gates * gate_grad, -1, keepdims=True))
    router_part = lax.dot_general(
        logit_back, normed_two.astype(F32), (((0,), (0,)), ((), ())), precision=HIGH
    )
    normed_two_back = expert_part + jnp.dot(logit_back, router_low.astype(F32).T, precision=HIGH)
    unit_two = hidden * scale_two
    weighted_two = normed_two_back * norm_gains[1]
    hidden_back = cotangent + scale_two * (
        weighted_two - unit_two * jnp.mean(weighted_two * unit_two, -1, keepdims=True)
    )
    gain_part_two = jnp.sum(normed_two_back * unit_two, 0)
    attention_back = jnp.concatenate(gather_tensor(hidden_back.astype(BF)), 0)
    output_grad = lax.dot_general(
        attention_back, attended, (((0,), (0,)), ((), ())), preferred_element_type=F32
    )
    attended_back = jnp.dot(attention_back, output_full, preferred_element_type=F32)
    attended_back = attended_back.astype(BF).reshape(group_rows, pair_heads, share_count, HD)
    key_grad = jnp.zeros((group_rows, pair_heads, HD), F32)
    value_grad = jnp.zeros((group_rows, pair_heads, HD), F32)
    query_blocks = []
    for block_index in range(block_total):
        row_start = block_index * block_rows
        scores, query_block = block_scores(row_start)
        probabilities = jnp.exp(scores - log_totals[block_index])
        back_block = attended_back[row_start : row_start + block_rows]
        prob_back = jnp.einsum(
            "qkgd,tkd->kgqt", back_block, value_rows, preferred_element_type=F32
        )
        inner_sum = jnp.sum(probabilities * prob_back, -1, keepdims=True)
        score_back = (probabilities * (prob_back - inner_sum)).astype(BF)
        query_blocks.append(
            score_scale
            * jnp.einsum("kgqt,tkd->qkgd", score_back, key_rows, preferred_element_type=F32)
        )
        key_grad = key_grad + score_scale * jnp.einsum(
            "kgqt,qkgd->tkd", score_back, query_block, preferred_element_type=F32
        )
        value_grad = value_grad + jnp.einsum(
            "kgqt,qkgd->tkd", probabilities.astype(BF), back_block, preferred_element_type=F32
        )
    query_grad_rows = jnp.concatenate(query_blocks, 0).reshape(group_rows, query_heads, HD)
    query_back = rotate(query_grad_rows, cosine, -sine_part).reshape(group_rows, query_wide)
    key_back = rotate(key_grad, cosine, -sine_part).reshape(group_rows, pair_wide)
    value_back = value_grad.reshape(group_rows, pair_wide)
    qkv_back = jnp.concatenate([query_back, key_back, value_back], 1).astype(BF)
    qkv_grad = lax.dot_general(
        rows_one, qkv_back, (((0,), (0,)), ((), ())), preferred_element_type=F32
    )
    normed_part = nt_dot(qkv_back, qkv_full)
    normed_one_back = scatter_tensor(
        [normed_part[b * local_rows : (b + 1) * local_rows] for b in range(X * C)]
    )
    gain_one = jnp.sum(normed_part * rows_one.astype(F32), 0, keepdims=True)
    gain_one = total_sum(gain_one) / norm_gains[:1]
    unit_one = stream * scale_one
    weighted_one = normed_one_back * norm_gains[0]
    stream_grad = hidden_back + scale_one * (
        weighted_one - unit_one * jnp.mean(weighted_one * unit_one, -1, keepdims=True)
    )

    def data_scatter(grad):
        wide = grad.shape[1]
        grad = grad.reshape(blocks, Z, Y, depth, wide).transpose(2, 1, 0, 3, 4)
        grad = grad.reshape(Y, Z, deep, wide)
        half = pick(grad, y, 0) + partner(pick(grad, 1 - y, 0).astype(BF), "y").astype(F32)
        total = pick(half, z, 0)
        for s in range(1, Z):
            total = total + partner(pick(half, z ^ s, 0).astype(BF), "z", s).astype(F32)
        if blocks > 1:
            total = lax.psum_scatter(total, "blk", scatter_dimension=0, tiled=True)
        return total

    output_owned = data_scatter(output_grad).T
    qkv_owned = data_scatter(qkv_grad)
    query_owned = qkv_owned[:, :query_wide]
    pair_owned = jnp.stack([qkv_owned[:, query_wide:first_pair], qkv_owned[:, first_pair:]])
    small = total_sum(jnp.concatenate([router_part, gain_part_two[None, :]], 0))
    router_grad = small[:experts].T
    gain_grad = jnp.concatenate([gain_one, small[experts:]], 0)
    rate_wide = 2.0 * D ** (-0.5)
    rate_output = 2.0 * max(1, 2 * H * HD // group_rows) ** (-0.5)
    rate_router = 2.0 * (4 * D) ** (-0.5)
    rate_down = 2.0 * (FF // 16) ** (-0.5)
    query_new = adam_update(
        query_weight, query_owned, query_moment, query_second, rate_wide, WEIGHT_DECAY
    )
    pair_new = adam_update(
        key_value_weight, pair_owned, key_value_moment, key_value_second, rate_wide, WEIGHT_DECAY
    )
    output_new = adam_update(
        output_weight, output_owned, output_moment, output_second, rate_output, WEIGHT_DECAY
    )
    router_new = adam_update(
        router_weight, router_grad, router_moment, router_second, rate_router, WEIGHT_DECAY
    )
    if blocks == 1:
        table = jnp.stack(
            [v for k in range(Z * C) for v in ((k % C) ^ c, (k // C) ^ z)]
        ).astype(jnp.int32)
        expert_new = expert_adam(
            table,
            owned,
            [gate_up_weight, gate_up_moment, gate_up_second],
            [down_weight, down_moment, down_second],
            rate_wide,
            rate_down,
        )
        gate_up_new, down_new = tuple(expert_new[:3]), tuple(expert_new[3:])
    else:
        placed = to_absolute(to_absolute(owned, "core", 0), "z", 1).transpose(1, 0, 2, 3, 4)
        placed = placed.reshape(experts, 3, LANES, LANES).astype(F32)
        gate_up_grad = lax.psum_scatter(
            placed[:, :2].transpose(1, 0, 2, 3), "blk", scatter_dimension=2, tiled=True
        )
        down_grad = lax.psum_scatter(placed[:, 2], "blk", scatter_dimension=2, tiled=True)
        gate_up_new = adam_update(
            gate_up_weight, gate_up_grad, gate_up_moment, gate_up_second, rate_wide, WEIGHT_DECAY
        )
        down_new = adam_update(
            down_weight, down_grad, down_moment, down_second, rate_down, WEIGHT_DECAY
        )
    gains_new = adam_update(norm_gains, gain_grad, gains_moment, gains_second, 0.2, 0.0)
    return (
        (result, stream_grad)
        + query_new
        + pair_new
        + output_new
        + router_new
        + gate_up_new
        + down_new
        + gains_new
    )


def solution(mesh):
    data_size, tensor_size = mesh.shape["dp"], mesh.shape["tensor"]
    blocks = data_size // (Z * Y)
    fine = Mesh(mesh.devices.reshape(blocks, Z, Y, tensor_size // C, C), EVERY)
    split = ("x", "core")
    rows = P(EVERY, None)
    wide = P(DATA, split)
    pair = P(None, DATA, split)
    tall = P(split, DATA)
    gate_up = P(None, None, DATA, split)
    down = P(None, split, DATA)
    group = P(DATA, None)
    return jax.shard_map(
        body,
        mesh=fine,
        in_specs=(rows, rows, group, group)
        + (wide,) * 3
        + (pair,) * 3
        + (tall,) * 3
        + (P(),) * 3
        + (gate_up,) * 3
        + (down,) * 3
        + (P(),) * 3,
        out_specs=(rows, rows)
        + (wide,) * 3
        + (pair,) * 3
        + (tall,) * 3
        + (P(),) * 3
        + (gate_up,) * 3
        + (down,) * 3
        + (P(),) * 3,
        check_vma=False,
    )
```
